512 devices in a mesh: ctx: 64 (over y_lo, x, z), exp: 8 (over y_hi, core).
Axes of the slice: x: 4, y: 8 (y_hi: 4, y_lo: 2; y = y_hi * 2 + y_lo), z: 8, core: 2. Of those that a mesh axis runs over, the one named last changes fastest.
Arguments:
- residual: bfloat16 [8192, 4096], P('ctx', 'exp'), may hold values from -6 to 6
- queries: bfloat16 [8192, 1024], P('ctx', 'exp'), may hold values from -9 to 9
- keys_values: bfloat16 [8192, 256], P('ctx'), may hold values from -9 to 9
- out_weight: bfloat16 [1024, 4096], P('exp', 'ctx'), may hold values from -0.5 to 0.5
- norm_gain: float32 [4096], replicated, may hold values from 0.25 to 1.75
- routes: int32 [8192, 8], P('ctx'), may hold values from 0 to 63, all different within a row; in each aligned block of 128 rows (0 to 127, 128 to 255, ...) at most 20 rows name the same one
- route_weights: float32 [8192, 8], P('ctx'), may hold values from 0.02 to 0.5
- gate_weight: bfloat16 [64, 4096, 1024], P('ctx', None, 'exp'), may hold values from -0.09375 to 0.09375
- up_weight: bfloat16 [64, 4096, 1024], P('ctx', None, 'exp'), may hold values from -0.09375 to 0.09375
- down_weight: bfloat16 [64, 1024, 4096], P('ctx', None, 'exp'), may hold values from -0.1875 to 0.1875
Outputs:
- layer_output: bfloat16 [8192, 4096], P('ctx', 'exp')
The draws below stay inside these ranges and needn't reach their ends.
Inputs may be any that keep to these rules, and one draw needn't show every extreme that they name: `routes`: each row names 8 different experts. Within the rows of one index of ctx (aligned blocks of 128 positions) no expert is named by more than 20 rows, a bound that some block reaches.
All inputs are finite; a program needn't handle non-finite values.
Results may differ from the reference program's by a relative error of at most 0.0058.
Values may be sent and summed in bfloat16 or wider, within the bound.
No kernel may reach another device: no remote copies, remote signals or barrier semaphores. Data moves between devices by JAX's collectives and lax.ppermute only.
A program may use at most 128 MiB of HBM per device.

```python
import math
import jax
import jax.numpy as jnp
import numpy as np
from jax import lax

D = 4096
HQ = 8
HD = 128
EFF = 1024
TOPK = 8
TOK_CTX = 128
SEQ = 8192
EXPERTS = 64
CAP = 20
N_CTX = 64


def draw_queries(key, part):
    key = jax.random.fold_in(key, 11)
    values = jnp.clip(jax.random.normal(key, (SEQ, HQ, HD), jnp.float32), -4.5, 4.5)
    return values.reshape(SEQ, HQ * HD).astype(jnp.bfloat16)


def draw_keys_values(key, part):
    key = jax.random.fold_in(key, 23)
    values = jnp.clip(jax.random.normal(key, (SEQ, 2 * HD), jnp.float32), -4.5, 4.5)
    return values.astype(jnp.bfloat16)


def block_scale(stream_key, shape, shards, smallest, top_value):
    loudness, own = 1.0, jax.random.fold_in(stream_key, 6)
    for dim, shards_of in shards:
        steps = jnp.exp(jax.random.uniform(jax.random.fold_in(own, dim), (shards_of,), jnp.float32, smallest / len(shards), top_value / len(shards)))
        loudness = loudness * jnp.repeat(steps, shape[dim] // shards_of).reshape([-1 if axis == dim else 1 for axis in range(len(shape))])
    return loudness


def deal_out(rng, own, number, rows, amount, top, limit, slope):
    ranking = jax.random.permutation(rng, amount)
    packed, common = load_shares(amount, rows * top, limit, slope, True), load_shares(amount, rows * top, limit, slope, False)
    places = jnp.arange(amount)

    def named(lengths, rotation):
        used = int((lengths > 0).sum())
        fixed = max(1, used // 4)
        passed = fixed + (places - fixed + rotation * (used - fixed)) % max(1, amount - fixed)
        return jnp.zeros((amount,), jnp.int32).at[ranking[jnp.where(places < fixed, places, passed)]].set(jnp.asarray(lengths, jnp.int32))

    lengths = jnp.where(number % 4 == 0, named(packed, number // 4), named(common, number - number // 4 - 1))
    mixed = jax.random.permutation(jax.random.fold_in(own, 3), amount)
    donor, sink = mixed[0:amount // 2 * 2:2], mixed[1:amount // 2 * 2:2]
    room = jnp.minimum(lengths[donor] - 1, limit - lengths[sink]) // 2
    room = jnp.where((donor == ranking[0]) | (sink == ranking[0]) | (lengths[sink] == 0), 0, jnp.maximum(room, 0))
    passed = jax.random.randint(jax.random.fold_in(own, 4), (amount // 2,), 0, 1 << 20) % (room + 1)
    lengths = lengths.at[donor].add(-passed).at[sink].add(passed)
    members = jnp.searchsorted(jnp.cumsum(lengths), jnp.arange(rows * top), side="right").astype(jnp.int32)
    listing = members.reshape(top, rows).T
    listing = listing[jax.random.permutation(jax.random.fold_in(own, 1), rows)]
    rotation = jax.random.randint(jax.random.fold_in(own, 2), (rows, 1), 0, top)
    return jnp.take_along_axis(listing, (jnp.arange(top)[None, :] + rotation) % top, axis=1)


def load_shares(amount, total, limit, skew, full):
    portions = [(1 << 20) // math.isqrt(standing ** skew) + 1 for standing in range(1, amount + 1)]
    largest = limit if full else min(limit, max(-(-total // amount), total * portions[0] // sum(portions)))
    least = 1 if total - largest >= amount - 1 else 0
    counts, spare = [largest] + [least] * (amount - 1), total - largest - least * (amount - 1)
    while spare > 0:
        movable = [i for i in range(1, amount) if counts[i] < largest] or [i for i in range(1, amount) if counts[i] < limit]
        pool, left = sum([portions[i] for i in movable]), spare
        for i in movable:
            extra = min(limit - counts[i], max(1, left * portions[i] // pool), spare)
            counts[i] = counts[i] + extra
            spare = spare - extra
    return np.array(counts)


def normal_values(rng, dims, spread, most, cuts=(), held_as=jnp.bfloat16):
    gain = block_scale(rng, dims, cuts, -0.22, 0.18) if cuts else 1.0
    drawn = jax.random.normal(rng, dims, jnp.float32) * spread * gain
    return jnp.minimum(jnp.maximum(drawn, -most), most).astype(held_as)


def setup_inputs(seed: int = 0) -> dict:
    key_list = jax.random.split(jax.random.key(seed), 11)
    residual = normal_values(key_list[0], (SEQ, D), 1.0, 6.0, ((0, 64), (1, 8)))
    queries = draw_queries(jax.random.fold_in(key_list[10], 71), 0)
    keys_values = draw_keys_values(jax.random.fold_in(key_list[10], 71), 0)
    out_weight = normal_values(key_list[3], (HQ * HD, D), (HQ * HD // 8) ** -0.5, 0.5, ((0, 8), (1, 64)))
    norm_gain = jnp.clip(1.0 + 0.15 * jax.random.normal(key_list[4], (D,), jnp.float32), 0.25, 1.75)
    routes_keys = jax.random.split(jax.random.fold_in(key_list[5], 1), SEQ // TOK_CTX)
    routes_turns = jax.random.permutation(jax.random.fold_in(key_list[5], 3), SEQ // TOK_CTX)
    routes = jax.vmap(lambda own, number: deal_out(jax.random.fold_in(key_list[5], 2), own, number, TOK_CTX, EXPERTS, TOPK, CAP, 2))(routes_keys, routes_turns).reshape((SEQ, TOPK))
    route_weights = jnp.clip(jnp.exp(math.log(0.5) - 3.218876 * jax.random.uniform(key_list[6], (SEQ, TOPK), jnp.float32) ** block_scale(key_list[6], (SEQ, TOPK), ((0, 64),), -0.2, 0.2)), 0.02, 0.5)
    gate_weight = normal_values(key_list[7], (EXPERTS, D, EFF), D ** -0.5, 0.09375, ((0, 64), (2, 8)))
    up_weight = normal_values(key_list[8], (EXPERTS, D, EFF), D ** -0.5, 0.09375, ((0, 64), (2, 8)))
    down_weight = normal_values(key_list[9], (EXPERTS, EFF, D), EFF ** -0.5, 0.1875, ((0, 64), (2, 8)))
    return dict(residual=residual, queries=queries, keys_values=keys_values, out_weight=out_weight, norm_gain=norm_gain, routes=routes, route_weights=route_weights, gate_weight=gate_weight, up_weight=up_weight, down_weight=down_weight)


def normalize(row_block, norm_gain):
    as_float = row_block.astype(jnp.float32)
    inv_rms = lax.rsqrt(lax.optimization_barrier(jnp.mean(as_float * as_float, axis=-1, keepdims=True)) + 1e-06)
    return (as_float * inv_rms * norm_gain.astype(jnp.float32)).astype(jnp.bfloat16)

def reference(residual, queries, keys_values, out_weight, norm_gain, routes, route_weights, gate_weight, up_weight, down_weight):
    query_heads = queries.astype(jnp.float32).reshape(SEQ, HQ, HD)
    key_rows = keys_values[:, :HD].astype(jnp.float32)
    value_rows = keys_values[:, HD:].astype(jnp.float32)
    position = jnp.arange(SEQ, dtype=jnp.int32)
    causal = position[None, :] <= position[:, None]

    def one_head(head_query):
        scores = jnp.dot(head_query, key_rows.T, precision=lax.Precision.HIGHEST) * HD ** (-0.5)
        scores = jnp.where(causal, scores, -1e+30)
        weights = jax.nn.softmax(scores, axis=-1)
        return jnp.dot(weights, value_rows, precision=lax.Precision.HIGHEST)
    head_outputs = lax.map(one_head, jnp.transpose(query_heads, (1, 0, 2)))
    attention = jnp.transpose(head_outputs, (1, 0, 2)).reshape(SEQ, HQ * HD).astype(jnp.bfloat16)
    mixed_rows = (residual.astype(jnp.float32) + jnp.dot(attention, out_weight, preferred_element_type=jnp.float32)).astype(jnp.bfloat16)
    normed = normalize(mixed_rows, norm_gain)
    flat_routes = routes.reshape(N_CTX, TOK_CTX * TOPK).astype(jnp.int32)
    onehot = (flat_routes[:, :, None] == jnp.arange(EXPERTS, dtype=jnp.int32)[None, None, :]).astype(jnp.int32)
    slot_index = lax.optimization_barrier(jnp.sum((jnp.cumsum(onehot, axis=1) - onehot) * onehot, axis=-1)).astype(jnp.int32)
    block_index = jnp.broadcast_to(jnp.arange(N_CTX, dtype=jnp.int32)[:, None], flat_routes.shape)
    token_index = (block_index * TOK_CTX + jnp.arange(TOK_CTX * TOPK, dtype=jnp.int32)[None, :] // TOPK).astype(jnp.int32)
    slot_table = jnp.full((EXPERTS, N_CTX, CAP), SEQ, jnp.int32).at[flat_routes, block_index, slot_index].set(token_index)
    padded = jnp.concatenate([normed, jnp.zeros((1, D), jnp.bfloat16)], axis=0)

    def one_expert(operands):
        table_rows, gate_matrix, up_matrix, down_matrix = operands
        expert_rows = padded[table_rows.reshape(-1)]
        gate_value = jnp.dot(expert_rows, gate_matrix, preferred_element_type=jnp.float32)
        up_value = jnp.dot(expert_rows, up_matrix, preferred_element_type=jnp.float32)
        hidden = (jax.nn.silu(gate_value) * up_value).astype(jnp.bfloat16)
        return jnp.dot(hidden, down_matrix, preferred_element_type=jnp.float32).astype(jnp.bfloat16)
    outputs = lax.map(one_expert, (slot_table, gate_weight, up_weight, down_weight))
    picked = outputs[flat_routes, (block_index * CAP + slot_index).astype(jnp.int32)]
    picked = picked.reshape(SEQ, TOPK, D).astype(jnp.float32)
    expert_sum = lax.optimization_barrier(jnp.sum(route_weights[:, :, None] * picked, axis=1))
    return (mixed_rows.astype(jnp.float32) + expert_sum).astype(jnp.bfloat16)
```

```python
import jax
import jax.numpy as jnp
import numpy as np
from jax import lax
from jax.experimental import pallas as pl
from jax.experimental.pallas import tpu as pltpu
from jax.sharding import Mesh
from jax.sharding import PartitionSpec as P

AXES = ("y_lo", "x", "z", "y_hi", "core")
CTX = ("y_lo", "x", "z")
YX = ("y_lo", "x")
EXP = ("y_hi", "core")
CAP = 20
HALF = CAP // 2
F32 = jnp.float32
BF16 = jnp.bfloat16
NEG = -1e30


def rounded(v):
    return lax.reduce_precision(v, 8, 7)


def split3(v):
    hi = rounded(v)
    mid = rounded(v - hi)
    low = v - hi - mid
    return hi.astype(BF16), mid.astype(BF16), low.astype(BF16)


def place_out_weight(columns):
    swap = [(p * 8 + e, e * 8 + p) for p in range(8) for e in range(8)]
    return lax.ppermute(columns, YX + EXP, swap)


def swap_cores(block):
    return lax.ppermute(block, "core", [(0, 1), (1, 0)])


def shift(block, step):
    return lax.ppermute(block, "y_hi", [(i, (i + step) % 4) for i in range(4)])


def own_first(block, axis):
    return jnp.where(lax.axis_index("core") == 0, block, jnp.flip(block, axis))


def near_weights(gate_weight, up_weight):
    row = lax.axis_index("y_hi")
    joined = jnp.concatenate([gate_weight, up_weight], axis=1).reshape(4, 2, 512, 256)
    joined = own_first(joined, 1).reshape(4, 1024, 256)
    return [lax.dynamic_index_in_dim(joined, (row + k) % 4, 0, keepdims=False) for k in (0, 1, 3, 2)]


def attention_rows(queries, keys_values, out_weight, down):
    tokens = queries.shape[0]
    ctx = lax.axis_index(CTX)
    part = lax.axis_index(EXP)
    rows = tokens // 8
    gathered = lax.all_gather(
        jnp.concatenate([queries, out_weight.T], axis=0), EXP, axis=0, tiled=False
    )
    all_queries = gathered[:, :tokens]
    columns = place_out_weight(gathered[:, tokens:])
    projection = lax.all_gather(columns, "z", axis=1, tiled=False)
    own = lax.dynamic_slice_in_dim(keys_values, part * rows, rows, axis=0)
    spread = jnp.broadcast_to(own[None], (64, rows, own.shape[1]))
    held = lax.all_to_all(spread, CTX, split_axis=0, concat_axis=0, tiled=True)
    keys = held[:, :, :128].reshape(64 * rows, 128)
    values = held[:, :, 128:].reshape(64 * rows, 128)
    scores = jnp.einsum("htd,kd->htk", all_queries, keys, preferred_element_type=F32) * (128**-0.5)
    key_index = jnp.arange(64 * rows, dtype=jnp.int32)
    key_position = (key_index // rows) * tokens + part * rows + key_index % rows
    position = ctx * tokens + jnp.arange(tokens, dtype=jnp.int32)
    visible = (key_position[None, :] <= position[:, None])[None]
    scores = jnp.where(visible, scores, NEG)
    top = jnp.max(scores, axis=-1)
    weights = jnp.where(visible, jnp.exp(scores - top[:, :, None]), 0.0)
    total = jnp.sum(weights, axis=-1)
    summed = jnp.einsum("htk,kd->htd", weights.astype(BF16), values, preferred_element_type=F32)
    seen = total > 0.0
    safe = jnp.where(seen, total, 1.0)
    mean = (summed / safe[:, :, None]).astype(BF16)
    level = jnp.where(seen, top + jnp.log(safe), NEG)
    hi, mid, low = split3(level)
    extra = jnp.stack([hi, mid, low] + [jnp.zeros_like(hi)] * 13, axis=1)
    sent = jnp.concatenate([mean, extra], axis=1)
    sent, down = lax.optimization_barrier((sent, down))
    down = jnp.concatenate([down, swap_cores(jnp.flip(down, 1))], axis=3).reshape(1024, 1024)
    came = lax.all_to_all(sent, EXP, split_axis=0, concat_axis=0, tiled=True)
    came_mean = came[:, :tokens].astype(F32)
    came_level = came[:, tokens : tokens + 3].astype(F32)
    came_level = came_level[:, 0] + (came_level[:, 1] + came_level[:, 2])
    share = jnp.exp(came_level - jnp.max(came_level, axis=0, keepdims=True))
    share = share / jnp.sum(share, axis=0, keepdims=True)
    mine = jnp.sum(came_mean * share[:, :, None], axis=0).astype(BF16)
    mine, down = lax.optimization_barrier((mine, down))
    attention = lax.all_gather(mine, EXP, axis=0, tiled=False)
    product = jnp.einsum("etr,ezcr->tzc", attention, projection, preferred_element_type=F32)
    return product.reshape(tokens, 512), down


def slot_tables(routes, route_weights):
    tokens = routes.shape[0]
    named = routes[:, :, None] == jnp.arange(64, dtype=jnp.int32)[None, None, :]
    member = jnp.any(named, axis=1)
    weight = jnp.sum(jnp.where(named, route_weights[:, :, None], 0.0), axis=1)
    order = jnp.arange(tokens, dtype=jnp.int32)
    earlier = (order[None, :] < order[:, None]).astype(BF16)
    rank = jnp.dot(earlier, member.astype(BF16), preferred_element_type=F32)
    slot = jnp.where(member, rank.astype(jnp.int32), -1).T
    here = lax.axis_index("core") * HALF + jnp.arange(HALF, dtype=jnp.int32)
    hit = slot[:, None, :] == here[None, :, None]
    onehot = hit.astype(BF16).reshape(64 * HALF, tokens)
    whole = jnp.where(hit, weight.T[:, None, :], 0.0).reshape(64 * HALF, tokens)
    high = rounded(whole)
    return onehot, jnp.concatenate([high, whole - high], axis=1).astype(BF16)


def kernel_call(body, outs, flops, moved, in_specs, vmem=24):
    whole = [pl.BlockSpec(shape, lambda i, n=len(shape): (0,) * n) for shape, _ in outs]
    return pl.pallas_call(
        body,
        grid=(1,),
        in_specs=in_specs,
        out_specs=whole,
        out_shape=[jax.ShapeDtypeStruct(shape, dtype) for shape, dtype in outs],
        compiler_params=pltpu.CompilerParams(vmem_limit_bytes=vmem * 1024 * 1024),
        cost_estimate=pl.CostEstimate(flops=flops, bytes_accessed=moved, transcendentals=0),
    )


def full(*shape):
    return pl.BlockSpec(shape, lambda i: (0,) * len(shape))


def page(k):
    return pl.BlockSpec((1, 1024, 256), lambda i: (k, 0, 0))


def dot(left, right):
    return jnp.dot(left, right, preferred_element_type=F32)


def receive_kernel(arrived, gain, low_weight, high_weight, scaled, squares, far_low, far_high):
    tiles = []
    for i in range(5):
        here = slice(128 * i, 128 * i + 128)
        rows = arrived[1024 * i : 1024 * i + 1024, :].astype(F32)
        rows = rows.reshape(128, 8, 128).reshape(128, 1024)
        block = (rows * gain[...]).astype(BF16)
        scaled[here, :] = block
        far_low[here, :] = dot(block, low_weight[...]).astype(BF16)
        far_high[here, :] = dot(block, high_weight[0]).astype(BF16)
        square = rows * rows
        total = square[:, :128]
        for j in range(1, 8):
            total = total + square[:, 128 * j : 128 * j + 128]
        total = jnp.sum(total.T, axis=0, keepdims=True)
        spread = total * 65537.0
        high = spread - (spread - total)
        tiles.append(jnp.concatenate([high, total - high], axis=1))
    tiles = jnp.concatenate(tiles + [jnp.zeros((11, 256), F32)], axis=0).astype(BF16)
    squares[...] = tiles
    far_low[640:656, :] = tiles


def near_kernel(
    scaled, squares, right_own, right_other, left_own, left_other, right_low, right_high, left_low, left_high
):
    for i in range(5):
        here = slice(128 * i, 128 * i + 128)
        block = scaled[here, :]
        right_low[here, :] = dot(block, right_own[...])
        right_high[here, :] = dot(block, right_other[0]).astype(BF16)
        left_low[here, :] = dot(block, left_own[...]).astype(BF16)
        left_high[here, :] = dot(block, left_other[0])
    right_low[640:656, :] = jnp.zeros((16, 256), F32)
    right_high[640:656, :] = squares[...]
    left_low[640:656, :] = squares[...]


def own_kernel(scaled, low_weight, high_weight, own):
    for i in range(5):
        here = slice(128 * i, 128 * i + 128)
        block = scaled[here, :]
        own[here, :256] = dot(block, low_weight[...])
        own[here, 256:] = dot(block, high_weight[0])


def hidden_kernel(own, squares, left_low, left_high, right_low, right_high, hidden):
    total = squares[...].astype(F32) + left_low[640:656, :].astype(F32)
    total = total + left_high[640:656, :].astype(F32) + right_low[640:656, :].astype(F32)
    total = total[:, :128] + total[:, 128:]
    for i in range(5):
        here = slice(128 * i, 128 * i + 128)
        scale = lax.rsqrt(total[i : i + 1, :] * (1.0 / 4096) + 1e-06)
        scale = jnp.broadcast_to(scale, (8, 128)).T[:, :1]
        for half, one, two in ((0, left_low, right_low), (1, left_high, right_high)):
            sums = own[here, 256 * half : 256 * half + 256]
            sums = (sums + one[here, :].astype(F32) + two[here, :].astype(F32)) * scale
            gate, up = sums[:, :128], sums[:, 128:]
            value = gate / (1.0 + jnp.exp(-gate)) * up
            hidden[half, here, :] = value.astype(BF16)


def expert_hidden(arrived, gain, pieces, swapped_near, swapped_far):
    weight = full(1024, 256)
    scaled, squares, far_low, far_high = kernel_call(
        receive_kernel,
        [((640, 1024), BF16), ((16, 256), BF16), ((656, 256), BF16), ((640, 256), BF16)],
        680_000_000,
        4_500_000,
        [full(5120, 128), full(1, 1024), weight, page(0)],
        60,
    )(arrived.reshape(5120, 128), gain[None], pieces[3], swapped_far)
    from_left = shift(far_low, 1)
    from_right = shift(far_high, -1)
    right_low, right_high, left_low, left_high = kernel_call(
        near_kernel,
        [((656, 256), F32), ((656, 256), BF16), ((656, 256), BF16), ((640, 256), F32)],
        1_400_000_000,
        5_500_000,
        [full(640, 1024), full(16, 256), weight, page(1), weight, page(2)],
    )(scaled, squares, pieces[1], swapped_near, pieces[2], swapped_near)
    came_left_high = shift(right_high, 1)
    came_right_low = shift(left_low, -1)
    came_left_low = shift((right_low + from_left.astype(F32)).astype(BF16), 1)
    came_right_high = shift((left_high + from_right.astype(F32)).astype(BF16), -1)
    own = kernel_call(
        own_kernel,
        [((640, 512), F32)],
        680_000_000,
        3_600_000,
        [full(640, 1024), weight, page(0)],
    )(scaled, pieces[0], swapped_near)[0]
    return kernel_call(
        hidden_kernel,
        [((2, 640, 128), BF16)],
        10_000_000,
        3_500_000,
        [full(640, 512), full(16, 256)] + [full(656, 256)] * 3 + [full(640, 256)],
    )(own, squares, came_left_low, came_left_high, came_right_low, came_right_high)[0]


def near_output_kernel(own, left, right, own_down, left_down, right_down, total):
    for i in range(5):
        here = slice(128 * i, 128 * i + 128)
        block = dot(own[0, here, :], own_down[:128, :]) + dot(own[1, here, :], own_down[128:, :])
        block = block + dot(left[0, here, :], left_down[:128, :])
        block = block + dot(left[1, here, :], left_down[128:, :])
        block = block + dot(right[0, here, :], right_down[:128, :])
        total[here, :] = block + dot(right[1, here, :], right_down[128:, :])


def final_kernel(total, far_low, far_high, weight, out):
    for i in range(5):
        here = slice(128 * i, 128 * i + 128)
        block = dot(far_low[here, :], weight[:128, :]) + dot(far_high[here, :], weight[128:, :])
        block = (total[here, :] + block).reshape(128, 8, 128)
        out[1024 * i : 1024 * i + 1024, :] = block.reshape(1024, 128).astype(BF16)


def expert_outputs(hidden, down):
    row = lax.axis_index("y_hi")

    def part(k):
        return lax.dynamic_slice_in_dim(down, (row + k) % 4 * 256, 256, axis=0)

    left = shift(hidden, 1)
    right = shift(hidden, -1)
    far_low = shift(left[0], 1)
    far_high = shift(right[1], -1)
    block, weight = full(2, 640, 128), full(256, 1024)
    total = kernel_call(
        near_output_kernel,
        [((640, 1024), F32)],
        1_000_000_000,
        5_000_000,
        [block, block, block, weight, weight, weight],
    )(hidden, left, right, part(0), part(3), part(1))[0]
    out = kernel_call(
        final_kernel,
        [((5120, 128), BF16)],
        340_000_000,
        5_000_000,
        [full(640, 1024), full(640, 128), full(640, 128), weight],
    )(total, far_low, far_high, part(2))[0]
    return out.reshape(64, 80, 128)


def per_device(
    residual,
    queries,
    keys_values,
    out_weight,
    norm_gain,
    routes,
    route_weights,
    gate_weight,
    up_weight,
    down_weight,
):
    tokens = queries.shape[0]
    row = lax.axis_index("y_hi")
    blocks = near_weights(gate_weight[0], up_weight[0])
    down = own_first(down_weight[0].reshape(4, 2, 128, 512), 1)
    attended, down = attention_rows(queries, keys_values, out_weight, down)
    attended, far = lax.optimization_barrier((attended, blocks[3]))
    far = shift(far, 2)
    mixed = (residual.astype(F32) + attended).astype(BF16)
    onehot, shares = slot_tables(routes, route_weights)
    chip_rows = jnp.concatenate([mixed, swap_cores(mixed)], axis=1)
    outgoing = jnp.dot(onehot, chip_rows, preferred_element_type=F32).astype(BF16)
    outgoing = outgoing.reshape(64, 80, 128)
    far, near = lax.optimization_barrier((far, (blocks[1], blocks[2])))
    pieces = [blocks[0], shift(near[1], -1), shift(near[0], 1), far]
    turned = jnp.flip(jnp.stack(pieces[:3]).reshape(3, 2, 512, 256), 1).reshape(3, 1024, 256)
    far_turned = jnp.flip(far.reshape(2, 512, 256), 0).reshape(1, 1024, 256)
    swapped = (swap_cores(turned), swap_cores(far_turned))
    arrived = lax.all_to_all(outgoing, CTX, split_axis=0, concat_axis=0, tiled=True)
    arrived, swapped = lax.optimization_barrier((arrived, swapped))
    gain = lax.dynamic_slice_in_dim(norm_gain, row * 1024, 1024)
    gain = own_first(gain.reshape(2, 512), 0).reshape(1024)
    hidden = expert_hidden(arrived, gain, pieces, *swapped)
    expert_out = expert_outputs(hidden, down)
    returned = lax.all_to_all(expert_out, CTX, split_axis=0, concat_axis=0, tiled=True)
    returned = returned.reshape(64 * HALF, 1024)
    sums = lax.dot_general(
        shares, returned, (((0,), (0,)), ((), ())), preferred_element_type=F32
    )
    sums = sums[:tokens] + sums[tokens:]
    return (mixed.astype(F32) + (sums[:, :512] + swap_cores(sums[:, 512:]))).astype(BF16)


def solution(mesh):
    fine = Mesh(mesh.devices.reshape(2, 4, 8, 4, 2), AXES)
    placed = (
        P(CTX, EXP),
        P(CTX, EXP),
        P(CTX, None),
        P(EXP, CTX),
        P(),
        P(CTX, None),
        P(CTX, None),
        P(CTX, None, EXP),
        P(CTX, None, EXP),
        P(CTX, None, EXP),
    )
    return jax.shard_map(
        per_device, mesh=fine, in_specs=placed, out_specs=P(CTX, EXP), check_vma=False
    )
```

```python
import jax
import jax.numpy as jnp
import numpy as np
from jax import lax
from jax.experimental import pallas as pl
from jax.experimental.pallas import tpu as pltpu
from jax.sharding import Mesh
from jax.sharding import PartitionSpec as P

AXES = ("y_lo", "x", "z", "y_hi", "core")
CTX = ("y_lo", "x", "z")
YX = ("y_lo", "x")
EXP = ("y_hi", "core")
CAP = 20
HALF = CAP // 2
F32 = jnp.float32
BF16 = jnp.bfloat16
NEG = -1e30


def rounded(v):
    return lax.reduce_precision(v, 8, 7)


def split3(v):
    hi = rounded(v)
    mid = rounded(v - hi)
    low = v - hi - mid
    return hi.astype(BF16), mid.astype(BF16), low.astype(BF16)


def place_out_weight(columns):
    swap = [(p * 8 + e, e * 8 + p) for p in range(8) for e in range(8)]
    return lax.ppermute(columns, YX + EXP, swap)


def swap_cores(block):
    return lax.ppermute(block, "core", [(0, 1), (1, 0)])


def shift(block, step):
    return lax.ppermute(block, "y_hi", [(i, (i + step) % 4) for i in range(4)])


def in_core_order(own, other, axis):
    first = lax.axis_index("core") == 0
    return jnp.concatenate(
        [jnp.where(first, own, other), jnp.where(first, other, own)], axis=axis
    )


def near_weights(gate_weight, up_weight):
    row = lax.axis_index("y_hi")
    joined = jnp.concatenate([gate_weight, up_weight], axis=1).reshape(4, 1024, 256)
    return [lax.dynamic_index_in_dim(joined, (row + k) % 4, 0, keepdims=False) for k in (0, 1, 3, 2)]


def attention_rows(queries, keys_values, out_weight, near):
    tokens = queries.shape[0]
    ctx = lax.axis_index(CTX)
    part = lax.axis_index(EXP)
    rows = tokens // 8
    gathered = lax.all_gather(
        jnp.concatenate([queries, out_weight.T], axis=0), EXP, axis=0, tiled=False
    )
    gathered, near = lax.optimization_barrier((gathered, near))
    near = [shift(near[0], 1), shift(near[1], -1)]
    all_queries = gathered[:, :tokens]
    columns = place_out_weight(gathered[:, tokens:])
    own = lax.dynamic_slice_in_dim(keys_values, part * rows, rows, axis=0)
    spread = jnp.broadcast_to(own[None], (64, rows, own.shape[1]))
    held = lax.all_to_all(spread, CTX, split_axis=0, concat_axis=0, tiled=True)
    keys = held[:, :, :128].reshape(64 * rows, 128)
    values = held[:, :, 128:].reshape(64 * rows, 128)
    scores = jnp.einsum("htd,kd->htk", all_queries, keys, preferred_element_type=F32) * (128**-0.5)
    key_index = jnp.arange(64 * rows, dtype=jnp.int32)
    key_position = (key_index // rows) * tokens + part * rows + key_index % rows
    position = ctx * tokens + jnp.arange(tokens, dtype=jnp.int32)
    visible = (key_position[None, :] <= position[:, None])[None]
    scores = jnp.where(visible, scores, NEG)
    top = jnp.max(scores, axis=-1)
    weights = jnp.where(visible, jnp.exp(scores - top[:, :, None]), 0.0)
    total = jnp.sum(weights, axis=-1)
    summed = jnp.einsum("htk,kd->htd", weights.astype(BF16), values, preferred_element_type=F32)
    seen = total > 0.0
    safe = jnp.where(seen, total, 1.0)
    mean = (summed / safe[:, :, None]).astype(BF16)
    level = jnp.where(seen, top + jnp.log(safe), NEG)
    hi, mid, low = split3(level)
    extra = jnp.stack([hi, mid, low] + [jnp.zeros_like(hi)] * 13, axis=1)
    sent = jnp.concatenate([mean, extra], axis=1)
    columns, _ = lax.optimization_barrier((columns, sent))
    projection = lax.all_gather(columns, "z", axis=1, tiled=False)
    came = lax.all_to_all(sent, EXP, split_axis=0, concat_axis=0, tiled=True)
    came_mean = came[:, :tokens].astype(F32)
    came_level = came[:, tokens : tokens + 3].astype(F32)
    came_level = came_level[:, 0] + (came_level[:, 1] + came_level[:, 2])
    share = jnp.exp(came_level - jnp.max(came_level, axis=0, keepdims=True))
    share = share / jnp.sum(share, axis=0, keepdims=True)
    mine = jnp.sum(came_mean * share[:, :, None], axis=0).astype(BF16)
    mine, near = lax.optimization_barrier((mine, near))
    attention = lax.all_gather(mine, EXP, axis=0, tiled=False)
    product = jnp.einsum("etr,ezcr->tzc", attention, projection, preferred_element_type=F32)
    return product.reshape(tokens, 512), near


def slot_tables(routes, route_weights):
    tokens = routes.shape[0]
    named = routes[:, :, None] == jnp.arange(64, dtype=jnp.int32)[None, None, :]
    member = jnp.any(named, axis=1)
    weight = jnp.sum(jnp.where(named, route_weights[:, :, None], 0.0), axis=1)
    order = jnp.arange(tokens, dtype=jnp.int32)
    earlier = (order[None, :] < order[:, None]).astype(BF16)
    rank = jnp.dot(earlier, member.astype(BF16), preferred_element_type=F32)
    slot = jnp.where(member, rank.astype(jnp.int32), -1).T
    here = lax.axis_index("core") * HALF + jnp.arange(HALF, dtype=jnp.int32)
    hit = slot[:, None, :] == here[None, :, None]
    onehot = hit.astype(BF16).reshape(64 * HALF, tokens)
    whole = jnp.where(hit, weight.T[:, None, :], 0.0).reshape(64 * HALF, tokens)
    high = rounded(whole)
    return onehot, jnp.concatenate([high, whole - high], axis=1).astype(BF16)


def kernel_call(body, outs, flops, moved, in_specs, vmem=24):
    whole = [pl.BlockSpec(shape, lambda i, n=len(shape): (0,) * n) for shape, _ in outs]
    return pl.pallas_call(
        body,
        grid=(1,),
        in_specs=in_specs,
        out_specs=whole,
        out_shape=[jax.ShapeDtypeStruct(shape, dtype) for shape, dtype in outs],
        compiler_params=pltpu.CompilerParams(vmem_limit_bytes=vmem * 1024 * 1024),
        cost_estimate=pl.CostEstimate(flops=flops, bytes_accessed=moved, transcendentals=0),
    )


def full(*shape):
    return pl.BlockSpec(shape, lambda i: (0,) * len(shape))


def dot(left, right):
    return jnp.dot(left, right, preferred_element_type=F32)


def receive_kernel(arrived, gain, low_weight, high_weight, scaled, squares, far_low, far_high):
    tiles = []
    for i in range(5):
        here = slice(128 * i, 128 * i + 128)
        rows = arrived[1024 * i : 1024 * i + 1024, :].astype(F32)
        rows = rows.reshape(128, 8, 128).reshape(128, 1024)
        block = (rows * gain[...]).astype(BF16)
        scaled[here, :] = block
        far_low[here, :] = dot(block, low_weight[...]).astype(BF16)
        far_high[here, :] = dot(block, high_weight[...]).astype(BF16)
        square = rows * rows
        total = square[:, :128]
        for j in range(1, 8):
            total = total + square[:, 128 * j : 128 * j + 128]
        total = jnp.sum(total.T, axis=0, keepdims=True)
        spread = total * 65537.0
        high = spread - (spread - total)
        tiles.append(jnp.concatenate([high, total - high], axis=1))
    tiles = jnp.concatenate(tiles + [jnp.zeros((11, 256), F32)], axis=0).astype(BF16)
    squares[...] = tiles
    far_low[640:656, :] = tiles


def near_kernel(
    scaled, squares, right_own, right_other, left_own, left_other, right_low, right_high, left_low, left_high
):
    for i in range(5):
        here = slice(128 * i, 128 * i + 128)
        block = scaled[here, :]
        right_low[here, :] = dot(block, right_own[...])
        right_high[here, :] = dot(block, right_other[...]).astype(BF16)
        left_low[here, :] = dot(block, left_own[...]).astype(BF16)
        left_high[here, :] = dot(block, left_other[...])
    right_low[640:656, :] = jnp.zeros((16, 256), F32)
    right_high[640:656, :] = squares[...]
    left_low[640:656, :] = squares[...]


def own_kernel(scaled, low_weight, high_weight, own):
    for i in range(5):
        here = slice(128 * i, 128 * i + 128)
        block = scaled[here, :]
        own[here, :256] = dot(block, low_weight[...])
        own[here, 256:] = dot(block, high_weight[...])


def hidden_kernel(own, squares, left_low, left_high, right_low, right_high, hidden):
    total = squares[...].astype(F32) + left_low[640:656, :].astype(F32)
    total = total + left_high[640:656, :].astype(F32) + right_low[640:656, :].astype(F32)
    total = total[:, :128] + total[:, 128:]
    for i in range(5):
        here = slice(128 * i, 128 * i + 128)
        scale = lax.rsqrt(total[i : i + 1, :] * (1.0 / 4096) + 1e-06)
        scale = jnp.broadcast_to(scale, (8, 128)).T[:, :1]
        for half, one, two in ((0, left_low, right_low), (1, left_high, right_high)):
            sums = own[here, 256 * half : 256 * half + 256]
            sums = (sums + one[here, :].astype(F32) + two[here, :].astype(F32)) * scale
            gate, up = sums[:, :128], sums[:, 128:]
            value = gate / (1.0 + jnp.exp(-gate)) * up
            hidden[half, here, :] = value.astype(BF16)


def expert_hidden(arrived, gain, low, high):
    weight = full(1024, 256)
    scaled, squares, far_low, far_high = kernel_call(
        receive_kernel,
        [((640, 1024), BF16), ((16, 256), BF16), ((656, 256), BF16), ((640, 256), BF16)],
        680_000_000,
        4_500_000,
        [full(5120, 128), full(1, 1024), weight, weight],
        60,
    )(arrived.reshape(5120, 128), gain[None], low[3], high[3])
    from_left = shift(far_low, 1)
    from_right = shift(far_high, -1)
    right_low, right_high, left_low, left_high = kernel_call(
        near_kernel,
        [((656, 256), F32), ((656, 256), BF16), ((656, 256), BF16), ((640, 256), F32)],
        1_400_000_000,
        5_500_000,
        [full(640, 1024), full(16, 256), weight, weight, weight, weight],
    )(scaled, squares, low[1], high[1], low[2], high[2])
    came_left_high = shift(right_high, 1)
    came_right_low = shift(left_low, -1)
    came_left_low = shift((right_low + from_left.astype(F32)).astype(BF16), 1)
    came_right_high = shift((left_high + from_right.astype(F32)).astype(BF16), -1)
    own = kernel_call(
        own_kernel,
        [((640, 512), F32)],
        680_000_000,
        3_600_000,
        [full(640, 1024), weight, weight],
    )(scaled, low[0], high[0])[0]
    return kernel_call(
        hidden_kernel,
        [((2, 640, 128), BF16)],
        10_000_000,
        3_500_000,
        [full(640, 512), full(16, 256)] + [full(656, 256)] * 3 + [full(640, 256)],
    )(own, squares, came_left_low, came_left_high, came_right_low, came_right_high)[0]


def near_output_kernel(own, left, right, own_down, left_down, right_down, total):
    for i in range(5):
        here = slice(128 * i, 128 * i + 128)
        block = dot(own[0, here, :], own_down[:128, :]) + dot(own[1, here, :], own_down[128:, :])
        block = block + dot(left[0, here, :], left_down[:128, :])
        block = block + dot(left[1, here, :], left_down[128:, :])
        block = block + dot(right[0, here, :], right_down[:128, :])
        total[here, :] = block + dot(right[1, here, :], right_down[128:, :])


def final_kernel(total, far_low, far_high, weight, out):
    for i in range(5):
        here = slice(128 * i, 128 * i + 128)
        block = dot(far_low[here, :], weight[:128, :]) + dot(far_high[here, :], weight[128:, :])
        block = (total[here, :] + block).reshape(128, 8, 128)
        out[1024 * i : 1024 * i + 1024, :] = block.reshape(1024, 128).astype(BF16)


def expert_outputs(hidden, down):
    row = lax.axis_index("y_hi")

    def part(k):
        return lax.dynamic_slice_in_dim(down, (row + k) % 4 * 256, 256, axis=0)

    left = shift(hidden, 1)
    right = shift(hidden, -1)
    far_low = shift(left[0], 1)
    far_high = shift(right[1], -1)
    block, weight = full(2, 640, 128), full(256, 1024)
    total = kernel_call(
        near_output_kernel,
        [((640, 1024), F32)],
        1_000_000_000,
        5_000_000,
        [block, block, block, weight, weight, weight],
    )(hidden, left, right, part(0), part(3), part(1))[0]
    out = kernel_call(
        final_kernel,
        [((5120, 128), BF16)],
        340_000_000,
        5_000_000,
        [full(640, 1024), full(640, 128), full(640, 128), weight],
    )(total, far_low, far_high, part(2))[0]
    return out.reshape(64, 80, 128)


def per_device(
    residual,
    queries,
    keys_values,
    out_weight,
    norm_gain,
    routes,
    route_weights,
    gate_weight,
    up_weight,
    down_weight,
):
    tokens = queries.shape[0]
    row = lax.axis_index("y_hi")
    first = lax.axis_index("core") == 0
    blocks = near_weights(gate_weight[0], up_weight[0])
    attended, near = attention_rows(
        queries, keys_values, out_weight, (blocks[1], blocks[2])
    )
    mixed = (residual.astype(F32) + attended).astype(BF16)
    mixed, near, far = lax.optimization_barrier((mixed, near, blocks[3]))
    onehot, shares = slot_tables(routes, route_weights)
    chip_rows = in_core_order(mixed, swap_cores(mixed), 1)
    outgoing = jnp.dot(onehot, chip_rows, preferred_element_type=F32).astype(BF16)
    outgoing = outgoing.reshape(64, 80, 128)
    pieces = [blocks[0], near[1], near[0], shift(far, 2)]
    swapped = swap_cores(jnp.stack(pieces))
    first = lax.axis_index("core") == 0
    low = [jnp.where(first, pieces[k], swapped[k]) for k in range(4)]
    high = [jnp.where(first, swapped[k], pieces[k]) for k in range(4)]
    down = in_core_order(down_weight[0], swap_cores(down_weight[0]), 1)
    arrived = lax.all_to_all(outgoing, CTX, split_axis=0, concat_axis=0, tiled=True)
    gain = lax.dynamic_slice_in_dim(norm_gain, row * 1024, 1024)
    hidden = expert_hidden(arrived, gain, low, high)
    expert_out = expert_outputs(hidden, down)
    returned = lax.all_to_all(expert_out, CTX, split_axis=0, concat_axis=0, tiled=True)
    returned = returned.reshape(64 * HALF, 1024)
    sums = lax.dot_general(
        shares, returned, (((0,), (0,)), ((), ())), preferred_element_type=F32
    )
    sums = sums[:tokens] + sums[tokens:]
    mine = jnp.where(first, sums[:, :512], sums[:, 512:])
    others = jnp.where(first, sums[:, 512:], sums[:, :512])
    return (mixed.astype(F32) + (mine + swap_cores(others))).astype(BF16)


def solution(mesh):
    fine = Mesh(mesh.devices.reshape(2, 4, 8, 4, 2), AXES)
    placed = (
        P(CTX, EXP),
        P(CTX, EXP),
        P(CTX, None),
        P(EXP, CTX),
        P(),
        P(CTX, None),
        P(CTX, None),
        P(CTX, None, EXP),
        P(CTX, None, EXP),
        P(CTX, None, EXP),
    )
    return jax.shard_map(
        per_device, mesh=fine, in_specs=placed, out_specs=P(CTX, EXP), check_vma=False
    )
```

```python
import jax
import jax.numpy as jnp
import numpy as np
from jax import lax
from jax.experimental import pallas as pl
from jax.experimental.pallas import tpu as pltpu
from jax.sharding import Mesh
from jax.sharding import PartitionSpec as P

AXES = ("y_lo", "x", "z", "y_hi", "core")
CTX = ("y_lo", "x", "z")
YX = ("y_lo", "x")
EXP = ("y_hi", "core")
CAP = 20
HALF = CAP // 2
F32 = jnp.float32
BF16 = jnp.bfloat16
NEG = -1e30


def rounded(v):
    return lax.reduce_precision(v, 8, 7)


def split3(v):
    hi = rounded(v)
    mid = rounded(v - hi)
    low = v - hi - mid
    return hi.astype(BF16), mid.astype(BF16), low.astype(BF16)


def place_out_weight(columns):
    swap = [(p * 8 + e, e * 8 + p) for p in range(8) for e in range(8)]
    return lax.ppermute(columns, YX + EXP, swap)


def swap_cores(block):
    return lax.ppermute(block, "core", [(0, 1), (1, 0)])


def shift(block, step):
    return lax.ppermute(block, "y_hi", [(i, (i + step) % 4) for i in range(4)])


def in_core_order(own, other, axis):
    first = lax.axis_index("core") == 0
    return jnp.concatenate(
        [jnp.where(first, own, other), jnp.where(first, other, own)], axis=axis
    )


def near_weights(gate_weight, up_weight):
    row = lax.axis_index("y_hi")
    joined = jnp.concatenate([gate_weight, up_weight], axis=1).reshape(4, 1024, 256)
    return [lax.dynamic_index_in_dim(joined, (row + k) % 4, 0, keepdims=False) for k in (0, 1, 3, 2)]


def attention_rows(queries, keys_values, out_weight, near):
    tokens = queries.shape[0]
    ctx = lax.axis_index(CTX)
    part = lax.axis_index(EXP)
    rows = tokens // 8
    gathered = lax.all_gather(
        jnp.concatenate([queries, out_weight.T], axis=0), EXP, axis=0, tiled=False
    )
    gathered, near = lax.optimization_barrier((gathered, near))
    near = [shift(near[0], 1), shift(near[1], -1)]
    all_queries = gathered[:, :tokens]
    columns = place_out_weight(gathered[:, tokens:])
    projection = lax.all_gather(columns, "z", axis=1, tiled=False)
    own = lax.dynamic_slice_in_dim(keys_values, part * rows, rows, axis=0)
    spread = jnp.broadcast_to(own[None], (64, rows, own.shape[1]))
    held = lax.all_to_all(spread, CTX, split_axis=0, concat_axis=0, tiled=True)
    keys = held[:, :, :128].reshape(64 * rows, 128)
    values = held[:, :, 128:].reshape(64 * rows, 128)
    scores = jnp.einsum("htd,kd->htk", all_queries, keys, preferred_element_type=F32) * (128**-0.5)
    key_index = jnp.arange(64 * rows, dtype=jnp.int32)
    key_position = (key_index // rows) * tokens + part * rows + key_index % rows
    position = ctx * tokens + jnp.arange(tokens, dtype=jnp.int32)
    visible = (key_position[None, :] <= position[:, None])[None]
    scores = jnp.where(visible, scores, NEG)
    top = jnp.max(scores, axis=-1)
    weights = jnp.where(visible, jnp.exp(scores - top[:, :, None]), 0.0)
    total = jnp.sum(weights, axis=-1)
    summed = jnp.einsum("htk,kd->htd", weights.astype(BF16), values, preferred_element_type=F32)
    seen = total > 0.0
    safe = jnp.where(seen, total, 1.0)
    mean = (summed / safe[:, :, None]).astype(BF16)
    level = jnp.where(seen, top + jnp.log(safe), NEG)
    hi, mid, low = split3(level)
    extra = jnp.stack([hi, mid, low] + [jnp.zeros_like(hi)] * 13, axis=1)
    sent = jnp.concatenate([mean, extra], axis=1)
    came = lax.all_to_all(sent, EXP, split_axis=0, concat_axis=0, tiled=True)
    came_mean = came[:, :tokens].astype(F32)
    came_level = came[:, tokens : tokens + 3].astype(F32)
    came_level = came_level[:, 0] + (came_level[:, 1] + came_level[:, 2])
    share = jnp.exp(came_level - jnp.max(came_level, axis=0, keepdims=True))
    share = share / jnp.sum(share, axis=0, keepdims=True)
    mine = jnp.sum(came_mean * share[:, :, None], axis=0).astype(BF16)
    mine, near = lax.optimization_barrier((mine, near))
    attention = lax.all_gather(mine, EXP, axis=0, tiled=False)
    product = jnp.einsum("etr,ezcr->tzc", attention, projection, preferred_element_type=F32)
    return product.reshape(tokens, 512), near


def slot_tables(routes, route_weights):
    tokens = routes.shape[0]
    named = routes[:, :, None] == jnp.arange(64, dtype=jnp.int32)[None, None, :]
    member = jnp.any(named, axis=1)
    weight = jnp.sum(jnp.where(named, route_weights[:, :, None], 0.0), axis=1)
    order = jnp.arange(tokens, dtype=jnp.int32)
    earlier = (order[None, :] < order[:, None]).astype(BF16)
    rank = jnp.dot(earlier, member.astype(BF16), preferred_element_type=F32)
    slot = jnp.where(member, rank.astype(jnp.int32), -1).T
    here = lax.axis_index("core") * HALF + jnp.arange(HALF, dtype=jnp.int32)
    hit = slot[:, None, :] == here[None, :, None]
    onehot = hit.astype(BF16).reshape(64 * HALF, tokens)
    whole = jnp.where(hit, weight.T[:, None, :], 0.0).reshape(64 * HALF, tokens)
    high = rounded(whole)
    return onehot, jnp.concatenate([high, whole - high], axis=1).astype(BF16)


def kernel_call(body, outs, flops, moved, in_specs, vmem=24):
    whole = [pl.BlockSpec(shape, lambda i, n=len(shape): (0,) * n) for shape, _ in outs]
    return pl.pallas_call(
        body,
        grid=(1,),
        in_specs=in_specs,
        out_specs=whole,
        out_shape=[jax.ShapeDtypeStruct(shape, dtype) for shape, dtype in outs],
        compiler_params=pltpu.CompilerParams(vmem_limit_bytes=vmem * 1024 * 1024),
        cost_estimate=pl.CostEstimate(flops=flops, bytes_accessed=moved, transcendentals=0),
    )


def full(*shape):
    return pl.BlockSpec(shape, lambda i: (0,) * len(shape))


def dot(left, right):
    return jnp.dot(left, right, preferred_element_type=F32)


def receive_kernel(arrived, gain, low_weight, high_weight, scaled, squares, far_low, far_high):
    tiles = []
    for i in range(5):
        here = slice(128 * i, 128 * i + 128)
        rows = arrived[1024 * i : 1024 * i + 1024, :].astype(F32)
        rows = rows.reshape(128, 8, 128).reshape(128, 1024)
        block = (rows * gain[...]).astype(BF16)
        scaled[here, :] = block
        far_low[here, :] = dot(block, low_weight[...]).astype(BF16)
        far_high[here, :] = dot(block, high_weight[...]).astype(BF16)
        square = rows * rows
        total = square[:, :128]
        for j in range(1, 8):
            total = total + square[:, 128 * j : 128 * j + 128]
        total = jnp.sum(total.T, axis=0, keepdims=True)
        spread = total * 65537.0
        high = spread - (spread - total)
        tiles.append(jnp.concatenate([high, total - high], axis=1))
    tiles = jnp.concatenate(tiles + [jnp.zeros((11, 256), F32)], axis=0).astype(BF16)
    squares[...] = tiles
    far_low[640:656, :] = tiles


def near_kernel(
    scaled, squares, right_own, right_other, left_own, left_other, right_low, right_high, left_low, left_high
):
    for i in range(5):
        here = slice(128 * i, 128 * i + 128)
        block = scaled[here, :]
        right_low[here, :] = dot(block, right_own[...])
        right_high[here, :] = dot(block, right_other[...]).astype(BF16)
        left_low[here, :] = dot(block, left_own[...]).astype(BF16)
        left_high[here, :] = dot(block, left_other[...])
    right_low[640:656, :] = jnp.zeros((16, 256), F32)
    right_high[640:656, :] = squares[...]
    left_low[640:656, :] = squares[...]


def own_kernel(scaled, low_weight, high_weight, own):
    for i in range(5):
        here = slice(128 * i, 128 * i + 128)
        block = scaled[here, :]
        own[here, :256] = dot(block, low_weight[...])
        own[here, 256:] = dot(block, high_weight[...])


def hidden_kernel(own, squares, left_low, left_high, right_low, right_high, hidden):
    total = squares[...].astype(F32) + left_low[640:656, :].astype(F32)
    total = total + left_high[640:656, :].astype(F32) + right_low[640:656, :].astype(F32)
    total = total[:, :128] + total[:, 128:]
    for i in range(5):
        here = slice(128 * i, 128 * i + 128)
        scale = lax.rsqrt(total[i : i + 1, :] * (1.0 / 4096) + 1e-06)
        scale = jnp.broadcast_to(scale, (8, 128)).T[:, :1]
        for half, one, two in ((0, left_low, right_low), (1, left_high, right_high)):
            sums = own[here, 256 * half : 256 * half + 256]
            sums = (sums + one[here, :].astype(F32) + two[here, :].astype(F32)) * scale
            gate, up = sums[:, :128], sums[:, 128:]
            value = gate / (1.0 + jnp.exp(-gate)) * up
            hidden[half, here, :] = value.astype(BF16)


def expert_hidden(arrived, gain, low, high):
    weight = full(1024, 256)
    scaled, squares, far_low, far_high = kernel_call(
        receive_kernel,
        [((640, 1024), BF16), ((16, 256), BF16), ((656, 256), BF16), ((640, 256), BF16)],
        680_000_000,
        4_500_000,
        [full(5120, 128), full(1, 1024), weight, weight],
        60,
    )(arrived.reshape(5120, 128), gain[None], low[3], high[3])
    from_left = shift(far_low, 1)
    from_right = shift(far_high, -1)
    right_low, right_high, left_low, left_high = kernel_call(
        near_kernel,
        [((656, 256), F32), ((656, 256), BF16), ((656, 256), BF16), ((640, 256), F32)],
        1_400_000_000,
        5_500_000,
        [full(640, 1024), full(16, 256), weight, weight, weight, weight],
    )(scaled, squares, low[1], high[1], low[2], high[2])
    came_left_high = shift(right_high, 1)
    came_right_low = shift(left_low, -1)
    came_left_low = shift((right_low + from_left.astype(F32)).astype(BF16), 1)
    came_right_high = shift((left_high + from_right.astype(F32)).astype(BF16), -1)
    own = kernel_call(
        own_kernel,
        [((640, 512), F32)],
        680_000_000,
        3_600_000,
        [full(640, 1024), weight, weight],
    )(scaled, low[0], high[0])[0]
    return kernel_call(
        hidden_kernel,
        [((2, 640, 128), BF16)],
        10_000_000,
        3_500_000,
        [full(640, 512), full(16, 256)] + [full(656, 256)] * 3 + [full(640, 256)],
    )(own, squares, came_left_low, came_left_high, came_right_low, came_right_high)[0]


def near_output_kernel(own, left, right, own_down, left_down, right_down, total):
    for i in range(5):
        here = slice(128 * i, 128 * i + 128)
        block = dot(own[0, here, :], own_down[:128, :]) + dot(own[1, here, :], own_down[128:, :])
        block = block + dot(left[0, here, :], left_down[:128, :])
        block = block + dot(left[1, here, :], left_down[128:, :])
        block = block + dot(right[0, here, :], right_down[:128, :])
        total[here, :] = block + dot(right[1, here, :], right_down[128:, :])


def final_kernel(total, far_low, far_high, weight, out):
    for i in range(5):
        here = slice(128 * i, 128 * i + 128)
        block = dot(far_low[here, :], weight[:128, :]) + dot(far_high[here, :], weight[128:, :])
        block = (total[here, :] + block).reshape(128, 8, 128)
        out[1024 * i : 1024 * i + 1024, :] = block.reshape(1024, 128).astype(BF16)


def expert_outputs(hidden, down):
    row = lax.axis_index("y_hi")

    def part(k):
        return lax.dynamic_slice_in_dim(down, (row + k) % 4 * 256, 256, axis=0)

    left = shift(hidden, 1)
    right = shift(hidden, -1)
    far_low = shift(left[0], 1)
    far_high = shift(right[1], -1)
    def product(block, k):
        rows = part(k)
        return dot(block[0], rows[:128]) + dot(block[1], rows[128:])

    total = product(hidden, 0) + product(left, 3) + product(right, 1)
    total = total + product((far_low, far_high), 2)
    return total.astype(BF16).reshape(64, 80, 128)


def per_device(
    residual,
    queries,
    keys_values,
    out_weight,
    norm_gain,
    routes,
    route_weights,
    gate_weight,
    up_weight,
    down_weight,
):
    tokens = queries.shape[0]
    row = lax.axis_index("y_hi")
    first = lax.axis_index("core") == 0
    blocks = near_weights(gate_weight[0], up_weight[0])
    attended, near = attention_rows(
        queries, keys_values, out_weight, (blocks[1], blocks[2])
    )
    mixed = (residual.astype(F32) + attended).astype(BF16)
    mixed, near, far = lax.optimization_barrier((mixed, near, blocks[3]))
    onehot, shares = slot_tables(routes, route_weights)
    chip_rows = in_core_order(mixed, swap_cores(mixed), 1)
    outgoing = jnp.dot(onehot, chip_rows, preferred_element_type=F32).astype(BF16)
    outgoing = outgoing.reshape(64, 80, 128)
    pieces = [blocks[0], near[1], near[0], shift(far, 2)]
    swapped = swap_cores(jnp.stack(pieces))
    first = lax.axis_index("core") == 0
    low = [jnp.where(first, pieces[k], swapped[k]) for k in range(4)]
    high = [jnp.where(first, swapped[k], pieces[k]) for k in range(4)]
    down = in_core_order(down_weight[0], swap_cores(down_weight[0]), 1)
    arrived = lax.all_to_all(outgoing, CTX, split_axis=0, concat_axis=0, tiled=True)
    gain = lax.dynamic_slice_in_dim(norm_gain, row * 1024, 1024)
    hidden = expert_hidden(arrived, gain, low, high)
    expert_out = expert_outputs(hidden, down)
    returned = lax.all_to_all(expert_out, CTX, split_axis=0, concat_axis=0, tiled=True)
    returned = returned.reshape(64 * HALF, 1024)
    sums = lax.dot_general(
        shares, returned, (((0,), (0,)), ((), ())), preferred_element_type=F32
    )
    sums = sums[:tokens] + sums[tokens:]
    mine = jnp.where(first, sums[:, :512], sums[:, 512:])
    others = jnp.where(first, sums[:, 512:], sums[:, :512])
    return (mixed.astype(F32) + (mine + swap_cores(others))).astype(BF16)


def solution(mesh):
    fine = Mesh(mesh.devices.reshape(2, 4, 8, 4, 2), AXES)
    placed = (
        P(CTX, EXP),
        P(CTX, EXP),
        P(CTX, None),
        P(EXP, CTX),
        P(),
        P(CTX, None),
        P(CTX, None),
        P(CTX, None, EXP),
        P(CTX, None, EXP),
        P(CTX, None, EXP),
    )
    return jax.shard_map(
        per_device, mesh=fine, in_specs=placed, out_specs=P(CTX, EXP), check_vma=False
    )
```

```python
import jax
import jax.numpy as jnp
import numpy as np
from jax import lax
from jax.experimental import pallas as pl
from jax.experimental.pallas import tpu as pltpu
from jax.sharding import Mesh
from jax.sharding import PartitionSpec as P

AXES = ("y_lo", "x", "z", "y_hi", "core")
CTX = ("y_lo", "x", "z")
YX = ("y_lo", "x")
EXP = ("y_hi", "core")
CAP = 20
HALF = CAP // 2
F32 = jnp.float32
BF16 = jnp.bfloat16
NEG = -1e30


def rounded(v):
    return lax.reduce_precision(v, 8, 7)


def split3(v):
    hi = rounded(v)
    mid = rounded(v - hi)
    low = v - hi - mid
    return hi.astype(BF16), mid.astype(BF16), low.astype(BF16)


def place_out_weight(columns):
    swap = [(p * 8 + e, e * 8 + p) for p in range(8) for e in range(8)]
    return lax.ppermute(columns, YX + EXP, swap)


def swap_cores(block):
    return lax.ppermute(block, "core", [(0, 1), (1, 0)])


def shift(block, step):
    return lax.ppermute(block, "y_hi", [(i, (i + step) % 4) for i in range(4)])


def in_core_order(own, other, axis):
    first = lax.axis_index("core") == 0
    return jnp.concatenate(
        [jnp.where(first, own, other), jnp.where(first, other, own)], axis=axis
    )


def near_weights(gate_weight, up_weight):
    row = lax.axis_index("y_hi")
    joined = jnp.concatenate([gate_weight, up_weight], axis=1).reshape(4, 1024, 256)
    return [lax.dynamic_index_in_dim(joined, (row + k) % 4, 0, keepdims=False) for k in (0, 1, 3, 2)]


def attention_rows(queries, keys_values, out_weight, near):
    tokens = queries.shape[0]
    ctx = lax.axis_index(CTX)
    part = lax.axis_index(EXP)
    rows = tokens // 8
    gathered = lax.all_gather(
        jnp.concatenate([queries, out_weight.T], axis=0), EXP, axis=0, tiled=False
    )
    gathered, near = lax.optimization_barrier((gathered, near))
    near = [shift(near[0], 1), shift(near[1], -1)]
    all_queries = gathered[:, :tokens]
    columns = place_out_weight(gathered[:, tokens:])
    projection = lax.all_gather(columns, "z", axis=1, tiled=False)
    own = lax.dynamic_slice_in_dim(keys_values, part * rows, rows, axis=0)
    spread = jnp.broadcast_to(own[None], (64, rows, own.shape[1]))
    held = lax.all_to_all(spread, CTX, split_axis=0, concat_axis=0, tiled=True)
    keys = held[:, :, :128].reshape(64 * rows, 128)
    values = held[:, :, 128:].reshape(64 * rows, 128)
    scores = jnp.einsum("htd,kd->htk", all_queries, keys, preferred_element_type=F32) * (128**-0.5)
    key_index = jnp.arange(64 * rows, dtype=jnp.int32)
    key_position = (key_index // rows) * tokens + part * rows + key_index % rows
    position = ctx * tokens + jnp.arange(tokens, dtype=jnp.int32)
    visible = (key_position[None, :] <= position[:, None])[None]
    scores = jnp.where(visible, scores, NEG)
    top = jnp.max(scores, axis=-1)
    weights = jnp.where(visible, jnp.exp(scores - top[:, :, None]), 0.0)
    total = jnp.sum(weights, axis=-1)
    summed = jnp.einsum("htk,kd->htd", weights.astype(BF16), values, preferred_element_type=F32)
    seen = total > 0.0
    safe = jnp.where(seen, total, 1.0)
    mean = (summed / safe[:, :, None]).astype(BF16)
    level = jnp.where(seen, top + jnp.log(safe), NEG)
    hi, mid, low = split3(level)
    extra = jnp.stack([hi, mid, low] + [jnp.zeros_like(hi)] * 13, axis=1)
    sent = jnp.concatenate([mean, extra], axis=1)
    came = lax.all_to_all(sent, EXP, split_axis=0, concat_axis=0, tiled=True)
    came_mean = came[:, :tokens].astype(F32)
    came_level = came[:, tokens : tokens + 3].astype(F32)
    came_level = came_level[:, 0] + (came_level[:, 1] + came_level[:, 2])
    share = jnp.exp(came_level - jnp.max(came_level, axis=0, keepdims=True))
    share = share / jnp.sum(share, axis=0, keepdims=True)
    mine = jnp.sum(came_mean * share[:, :, None], axis=0).astype(BF16)
    mine, near = lax.optimization_barrier((mine, near))
    attention = lax.all_gather(mine, EXP, axis=0, tiled=False)
    product = jnp.einsum("etr,ezcr->tzc", attention, projection, preferred_element_type=F32)
    return product.reshape(tokens, 512), near


def slot_tables(routes, route_weights):
    tokens = routes.shape[0]
    named = routes[:, :, None] == jnp.arange(64, dtype=jnp.int32)[None, None, :]
    member = jnp.any(named, axis=1)
    weight = jnp.sum(jnp.where(named, route_weights[:, :, None], 0.0), axis=1)
    order = jnp.arange(tokens, dtype=jnp.int32)
    earlier = (order[None, :] < order[:, None]).astype(BF16)
    rank = jnp.dot(earlier, member.astype(BF16), preferred_element_type=F32)
    slot = jnp.where(member, rank.astype(jnp.int32), -1).T
    here = lax.axis_index("core") * HALF + jnp.arange(HALF, dtype=jnp.int32)
    hit = slot[:, None, :] == here[None, :, None]
    onehot = hit.astype(BF16).reshape(64 * HALF, tokens)
    whole = jnp.where(hit, weight.T[:, None, :], 0.0).reshape(64 * HALF, tokens)
    high = rounded(whole)
    return onehot, jnp.concatenate([high, whole - high], axis=1).astype(BF16)


def kernel_call(body, outs, flops, moved, in_specs, vmem=24):
    whole = [pl.BlockSpec(shape, lambda i, n=len(shape): (0,) * n) for shape, _ in outs]
    return pl.pallas_call(
        body,
        grid=(1,),
        in_specs=in_specs,
        out_specs=whole,
        out_shape=[jax.ShapeDtypeStruct(shape, dtype) for shape, dtype in outs],
        compiler_params=pltpu.CompilerParams(vmem_limit_bytes=vmem * 1024 * 1024),
        cost_estimate=pl.CostEstimate(flops=flops, bytes_accessed=moved, transcendentals=0),
    )


def full(*shape):
    return pl.BlockSpec(shape, lambda i: (0,) * len(shape))


def dot(left, right):
    return jnp.dot(left, right, preferred_element_type=F32)


def receive_kernel(arrived, gain, low_weight, high_weight, scaled, squares, far_low, far_high):
    tiles = []
    for i in range(5):
        here = slice(128 * i, 128 * i + 128)
        rows = arrived[1024 * i : 1024 * i + 1024, :].astype(F32).reshape(128, 8, 128)
        total = jnp.sum(rows * rows, axis=1)
        block = (rows.reshape(128, 1024) * gain[...]).astype(BF16)
        scaled[here, :] = block
        far_low[here, :] = dot(block, low_weight[...]).astype(BF16)
        far_high[here, :] = dot(block, high_weight[...]).astype(BF16)
        total = jnp.sum(total.T, axis=0, keepdims=True)
        spread = total * 65537.0
        high = spread - (spread - total)
        tiles.append(jnp.concatenate([high, total - high], axis=1))
    tiles = jnp.concatenate(tiles + [jnp.zeros((11, 256), F32)], axis=0).astype(BF16)
    squares[...] = tiles
    far_low[640:656, :] = tiles


def near_kernel(
    scaled, squares, right_own, right_other, left_own, left_other, right_low, right_high, left_low, left_high
):
    for i in range(5):
        here = slice(128 * i, 128 * i + 128)
        block = scaled[here, :]
        right_low[here, :] = dot(block, right_own[...])
        right_high[here, :] = dot(block, right_other[...]).astype(BF16)
        left_low[here, :] = dot(block, left_own[...]).astype(BF16)
        left_high[here, :] = dot(block, left_other[...])
    right_low[640:656, :] = jnp.zeros((16, 256), F32)
    right_high[640:656, :] = squares[...]
    left_low[640:656, :] = squares[...]


def own_kernel(scaled, low_weight, high_weight, own):
    for i in range(5):
        here = slice(128 * i, 128 * i + 128)
        block = scaled[here, :]
        own[here, :256] = dot(block, low_weight[...])
        own[here, 256:] = dot(block, high_weight[...])


def hidden_kernel(own, squares, left_low, left_high, right_low, right_high, hidden):
    total = squares[...].astype(F32) + left_low[640:656, :].astype(F32)
    total = total + left_high[640:656, :].astype(F32) + right_low[640:656, :].astype(F32)
    total = total[:, :128] + total[:, 128:]
    for i in range(5):
        here = slice(128 * i, 128 * i + 128)
        scale = lax.rsqrt(total[i : i + 1, :] * (1.0 / 4096) + 1e-06)
        scale = jnp.broadcast_to(scale, (8, 128)).T[:, :1]
        for half, one, two in ((0, left_low, right_low), (1, left_high, right_high)):
            sums = own[here, 256 * half : 256 * half + 256]
            sums = (sums + one[here, :].astype(F32) + two[here, :].astype(F32)) * scale
            gate, up = sums[:, :128], sums[:, 128:]
            value = gate / (1.0 + jnp.exp(-gate)) * up
            hidden[half, here, :] = value.astype(BF16)


def expert_hidden(arrived, gain, low, high, down):
    weight = full(1024, 256)
    scaled, squares, far_low, far_high = kernel_call(
        receive_kernel,
        [((640, 1024), BF16), ((16, 256), BF16), ((656, 256), BF16), ((640, 256), BF16)],
        680_000_000,
        4_500_000,
        [full(5120, 128), full(1, 1024), weight, weight],
        60,
    )(arrived.reshape(5120, 128), gain[None], low[3], high[3])
    from_left = shift(far_low, 1)
    from_right = shift(far_high, -1)
    right_low, right_high, left_low, left_high = kernel_call(
        near_kernel,
        [((656, 256), F32), ((656, 256), BF16), ((656, 256), BF16), ((640, 256), F32)],
        1_400_000_000,
        5_500_000,
        [full(640, 1024), full(16, 256), weight, weight, weight, weight],
    )(scaled, squares, low[1], high[1], low[2], high[2])
    down, _ = lax.optimization_barrier((down, left_high))
    down = in_core_order(*down, 1)
    came_left_high = shift(right_high, 1)
    came_right_low = shift(left_low, -1)
    came_left_low = shift((right_low + from_left.astype(F32)).astype(BF16), 1)
    came_right_high = shift((left_high + from_right.astype(F32)).astype(BF16), -1)
    own = kernel_call(
        own_kernel,
        [((640, 512), F32)],
        680_000_000,
        3_600_000,
        [full(640, 1024), weight, weight],
    )(scaled, low[0], high[0])[0]
    hidden = kernel_call(
        hidden_kernel,
        [((2, 640, 128), BF16)],
        10_000_000,
        3_500_000,
        [full(640, 512), full(16, 256)] + [full(656, 256)] * 3 + [full(640, 256)],
    )(own, squares, came_left_low, came_left_high, came_right_low, came_right_high)[0]
    return hidden, down


def near_output_kernel(own, left, right, own_down, left_down, right_down, total):
    for i in range(5):
        here = slice(128 * i, 128 * i + 128)
        block = dot(own[0, here, :], own_down[:128, :]) + dot(own[1, here, :], own_down[128:, :])
        block = block + dot(left[0, here, :], left_down[:128, :])
        block = block + dot(left[1, here, :], left_down[128:, :])
        block = block + dot(right[0, here, :], right_down[:128, :])
        total[here, :] = block + dot(right[1, here, :], right_down[128:, :])


def final_kernel(total, far_low, far_high, weight, out):
    for i in range(5):
        here = slice(128 * i, 128 * i + 128)
        block = dot(far_low[here, :], weight[:128, :]) + dot(far_high[here, :], weight[128:, :])
        block = (total[here, :] + block).reshape(128, 8, 128)
        out[1024 * i : 1024 * i + 1024, :] = block.reshape(1024, 128).astype(BF16)


def expert_outputs(hidden, down):
    row = lax.axis_index("y_hi")

    def part(k):
        return lax.dynamic_slice_in_dim(down, (row + k) % 4 * 256, 256, axis=0)

    left = shift(hidden, 1)
    right = shift(hidden, -1)
    far_low = shift(left[0], 1)
    far_high = shift(right[1], -1)
    def product(block, k):
        rows = part(k)
        return dot(block[0], rows[:128]) + dot(block[1], rows[128:])

    total = product(hidden, 0) + product(left, 3) + product(right, 1)
    total = total + product((far_low, far_high), 2)
    return total.astype(BF16).reshape(64, 80, 128)


def per_device(
    residual,
    queries,
    keys_values,
    out_weight,
    norm_gain,
    routes,
    route_weights,
    gate_weight,
    up_weight,
    down_weight,
):
    tokens = queries.shape[0]
    row = lax.axis_index("y_hi")
    first = lax.axis_index("core") == 0
    blocks = near_weights(gate_weight[0], up_weight[0])
    attended, near = attention_rows(
        queries, keys_values, out_weight, (blocks[1], blocks[2])
    )
    mixed = (residual.astype(F32) + attended).astype(BF16)
    mixed, near, far = lax.optimization_barrier((mixed, near, blocks[3]))
    onehot, shares = slot_tables(routes, route_weights)
    chip_rows = in_core_order(mixed, swap_cores(mixed), 1)
    outgoing = jnp.dot(onehot, chip_rows, preferred_element_type=F32).astype(BF16)
    outgoing = outgoing.reshape(64, 80, 128)
    pieces = [blocks[0], near[1], near[0], shift(far, 2)]
    swapped = swap_cores(jnp.stack(pieces))
    first = lax.axis_index("core") == 0
    low = [jnp.where(first, pieces[k], swapped[k]) for k in range(4)]
    high = [jnp.where(first, swapped[k], pieces[k]) for k in range(4)]
    down = (down_weight[0], swap_cores(down_weight[0]))
    arrived = lax.all_to_all(outgoing, CTX, split_axis=0, concat_axis=0, tiled=True)
    gain = lax.dynamic_slice_in_dim(norm_gain, row * 1024, 1024)
    hidden, down = expert_hidden(arrived, gain, low, high, down)
    expert_out = expert_outputs(hidden, down)
    returned = lax.all_to_all(expert_out, CTX, split_axis=0, concat_axis=0, tiled=True)
    returned = returned.reshape(64 * HALF, 1024)
    sums = lax.dot_general(
        shares, returned, (((0,), (0,)), ((), ())), preferred_element_type=F32
    )
    sums = sums[:tokens] + sums[tokens:]
    mine = jnp.where(first, sums[:, :512], sums[:, 512:])
    others = jnp.where(first, sums[:, 512:], sums[:, :512])
    return (mixed.astype(F32) + (mine + swap_cores(others))).astype(BF16)


def solution(mesh):
    fine = Mesh(mesh.devices.reshape(2, 4, 8, 4, 2), AXES)
    placed = (
        P(CTX, EXP),
        P(CTX, EXP),
        P(CTX, None),
        P(EXP, CTX),
        P(),
        P(CTX, None),
        P(CTX, None),
        P(CTX, None, EXP),
        P(CTX, None, EXP),
        P(CTX, None, EXP),
    )
    return jax.shard_map(
        per_device, mesh=fine, in_specs=placed, out_specs=P(CTX, EXP), check_vma=False
    )
```
